128 devices in a mesh: shard: 32 (over z, x_hi, y), rep: 4 (over x_lo, core).
Axes of the slice: x: 4 (x_hi: 2, x_lo: 2; x = x_hi * 2 + x_lo), y: 4, z: 4, core: 2. Of those that a mesh axis runs over, the one named last changes fastest.
Arguments:
- weights: bfloat16 [6144, 196608], P('rep', 'shard'), may hold values from -12 to 12
- keep_mask: int32 [48, 1536], P('rep', 'shard'), may hold values from 0 to 1, as said below
- test_matrix: bfloat16 [196608, 128], P('shard'), may hold values from -6 to 6
Outputs:
- range_basis: float32 [6144, 128], P('rep')
- projection: float32 [196608, 128], P(('shard', 'rep'))
The draws below stay inside these ranges and needn't reach their ends.
Inputs may be any that keep to these rules, and one draw needn't show every extreme that they name: `keep_mask`: each device's 12 x 48 blocks hold at most 144 kept blocks, and some device holds exactly 144; every device holds at least one; all devices of one column shard hold equally many.
All inputs are finite; a program needn't handle non-finite values.
Results may differ from the reference program's by a relative error of at most 0.0028.
Values sent between devices are 32-bit elements; how exact they have to be, the bound alone decides.
No kernel may reach another device: no remote copies, remote signals or barrier semaphores. Data moves between devices by JAX's collectives and lax.ppermute only.
A program may use at most 128 MiB of HBM per device.

```python
import math
import jax
import jax.numpy as jnp
from jax import lax

D = 6144
K = 128
BLOCK = 128
CB_DEV = 48
TILE_MOST = 144
COLUMNS = 196608
N_SHARD = 32
N_REP = 4


def draw_keep_mask(key, part):
    key = jax.random.fold_in(key, 11)
    row_blocks = D // BLOCK // N_REP
    total_tiles = row_blocks * CB_DEV
    key_shift, key_heavy, key_order = jax.random.split(key, 3)
    shifts = jax.random.randint(key_shift, (N_SHARD,), 0, 4)
    heaviest = jax.random.randint(key_heavy, (), 0, N_SHARD)
    shifts = jnp.where(jnp.arange(N_SHARD) == heaviest, 0, shifts)
    kept_counts = jnp.maximum(jnp.right_shift(jnp.full((N_SHARD,), TILE_MOST, jnp.int32), shifts.astype(jnp.int32)), 1)
    order_keys = jax.random.split(key_order, N_REP * N_SHARD)
    orders = jax.vmap(lambda one_key: jax.random.permutation(one_key, total_tiles))(order_keys)
    orders = orders.reshape(N_REP, N_SHARD, total_tiles).astype(jnp.int32)
    kept = (orders < kept_counts[None, :, None]).astype(jnp.int32)
    kept = kept.reshape(N_REP, N_SHARD, row_blocks, CB_DEV).transpose(0, 2, 1, 3)
    return kept.reshape(N_REP * row_blocks, N_SHARD * CB_DEV)


def level_of(stream_key, dims, cuts, least, top_value):
    level = 1.0
    for dim, blocks in cuts:
        heights = jax.random.uniform(jax.random.fold_in(jax.random.fold_in(stream_key, 6), dim), (blocks,), jnp.float32, least / len(cuts), top_value / len(cuts))
        level = level * jnp.repeat(jnp.exp(heights), dims[dim] // blocks).reshape((-1,) + (1,) * (len(dims) - 1 - dim))
    return level


def scatter_about(key, extent, deviation, bound, cuts=(), held_as=jnp.bfloat16):
    loudness = level_of(key, extent, cuts, -0.22, 0.18) if cuts else 1.0
    entries = jax.random.normal(key, extent, jnp.float32) * deviation * loudness
    return jnp.minimum(jnp.maximum(entries, -bound), bound).astype(held_as)


def setup_inputs(seed: int = 0) -> dict:
    key_of = jax.random.split(jax.random.key(seed), 4)
    weights = scatter_about(key_of[0], (D, COLUMNS), 2.0, 12.0, ((0, 4), (1, 32)))
    keep_mask = draw_keep_mask(jax.random.fold_in(key_of[3], 71), 0)
    test_matrix = scatter_about(key_of[2], (COLUMNS, K), 1.0, 6.0, ((0, 32),))
    return {"weights": weights, "keep_mask": keep_mask, "test_matrix": test_matrix}


def reference(weights, keep_mask, test_matrix):
    panel_width = CB_DEV * BLOCK
    panel_count = COLUMNS // panel_width
    row_blocks = D // BLOCK
    indices = jnp.arange(panel_count, dtype=jnp.int32)

    def panel(index):
        columns = lax.dynamic_slice_in_dim(weights, (index * panel_width).astype(jnp.int32), panel_width, 1)
        marks = lax.dynamic_slice_in_dim(keep_mask, (index * CB_DEV).astype(jnp.int32), CB_DEV, 1)
        blocked = columns.reshape(row_blocks, BLOCK, CB_DEV, BLOCK) * marks[:, None, :, None].astype(columns.dtype)
        return blocked.reshape(D, panel_width)

    def add_sketch(total, index):
        test_rows = lax.dynamic_slice_in_dim(test_matrix, (index * panel_width).astype(jnp.int32), panel_width, 0)
        return (total + jnp.dot(panel(index).astype(jnp.float32), test_rows.astype(jnp.float32), preferred_element_type=jnp.float32), None)
    sketch, unused = lax.scan(add_sketch, jnp.zeros((D, K), jnp.float32), indices)
    gram_matrix = lax.dot_general(sketch, sketch, (((0,), (0,)), ((), ())), precision=lax.Precision.HIGHEST)
    factor = jnp.linalg.cholesky(gram_matrix)
    basis = lax.linalg.triangular_solve(factor, sketch, left_side=False, lower=True, transpose_a=True)
    basis_low = basis.astype(jnp.bfloat16)

    def project(index):
        return lax.dot_general(panel(index).astype(jnp.float32), basis_low.astype(jnp.float32), (((0,), (0,)), ((), ())), preferred_element_type=jnp.float32)
    projection = lax.map(project, indices).reshape(COLUMNS, K)
    return (basis * math.sqrt(D), projection)
```

```python
import itertools
import math

import jax
import jax.numpy as jnp
from jax import lax
from jax.experimental import pallas as pl
from jax.experimental.pallas import tpu as pltpu
from jax.sharding import PartitionSpec as P

D = 6144
K = 128
BLOCK = 128
ROWS = 1536
WIDTH = 6144
QUARTER = ROWS // 4
SUB = QUARTER // 4
PANEL = 1536
TILE = 256
AXES = ("shard", "rep")
HIGHEST = lax.Precision.HIGHEST

FOLD_A, FOLD_B = (1, 0, 3, 2), (3, 2, 1, 0)
LABEL_A, LABEL_B = (0, 1, 1, 0), (0, 0, 1, 1)


def device(z, x_hi, y, x_lo, core):
    return ((z * 2 + x_hi) * 4 + y) * 4 + x_lo * 2 + core


PLACES = list(itertools.product(range(4), range(2), range(4), range(2), range(2)))


def pairs(partner):
    return [(device(*place), device(*partner(*place))) for place in PLACES]


def square(first, bits):
    def partner(z, x_hi, y, x_lo, core):
        fold = FOLD_A if (core == 0) == first else FOLD_B
        return (fold[z] if bits & 1 else z, x_hi, fold[y] if bits & 2 else y, x_lo, core)

    return pairs(partner)


ACROSS = pairs(lambda z, x_hi, y, x_lo, core: (z, 1 - x_hi, y, x_lo, core))
CORES = pairs(lambda z, x_hi, y, x_lo, core: (z, x_hi, y, x_lo, 1 - core))
CHIPS = pairs(lambda z, x_hi, y, x_lo, core: (z, x_hi, y, 1 - x_lo, core))


def swap(value, perm):
    return lax.ppermute(value, AXES, perm)


def label(table, place):
    return sum(jnp.where(place == i, v, 0) for i, v in enumerate(table) if v)


def position():
    shard, rep = lax.axis_index("shard"), lax.axis_index("rep")
    y, z = lax.rem(shard, 4), shard // 8
    core, x_lo = lax.rem(rep, 2), rep // 2
    a = 2 * label(LABEL_A, y) + label(LABEL_A, z)
    b = 2 * label(LABEL_B, y) + label(LABEL_B, z)
    return jnp.stack([jnp.where(core == 0, a, b), jnp.where(core == 0, b, a), x_lo, core]).astype(jnp.int32)


def masked(tile, keep, row_block, col_block):
    rows, cols = tile.shape
    return jnp.concatenate(
        [
            jnp.concatenate(
                [
                    tile[r * BLOCK : (r + 1) * BLOCK, c * BLOCK : (c + 1) * BLOCK]
                    * keep[row_block + r, col_block + c].astype(jnp.float32).astype(tile.dtype)
                    for c in range(cols // BLOCK)
                ],
                axis=1,
            )
            for r in range(rows // BLOCK)
        ],
        axis=0,
    )


def sketch_kernel(first, place, keep, weights, test, *rest):
    outs, total = rest[:2], rest[2]
    panel, which = pl.program_id(0), pl.program_id(1)
    quarter = place[0] ^ (first + which)
    tile = masked(weights[...], keep, quarter * (QUARTER // BLOCK), panel * (PANEL // BLOCK))
    part = jnp.dot(tile, test[...], preferred_element_type=jnp.float32)

    @pl.when(panel == 0)
    def _():
        total[which] = part

    @pl.when(panel > 0)
    def _():
        total[which] += part

    @pl.when(panel == WIDTH // PANEL - 1)
    def _():
        for i, out in enumerate(outs):

            @pl.when(which == i)
            def _():
                for m in range(4):
                    start = pl.multiple_of((place[1] ^ m) * SUB, 8)
                    out[m * SUB : (m + 1) * SUB, :] = total[i, pl.ds(start, SUB), :]


def sketch_parts(first, place, keep_mask, weights, test_matrix):
    return pl.pallas_call(
        lambda *refs: sketch_kernel(first, *refs),
        grid_spec=pltpu.PrefetchScalarGridSpec(
            num_scalar_prefetch=2,
            grid=(WIDTH // PANEL, 2),
            in_specs=[
                pl.BlockSpec((QUARTER, PANEL), lambda j, k, place, keep: (place[0] ^ (first + k), j)),
                pl.BlockSpec((PANEL, K), lambda j, k, place, keep: (j, 0)),
            ],
            out_specs=[pl.BlockSpec((QUARTER, K), lambda j, k, place, keep: (0, 0))] * 2,
            scratch_shapes=[pltpu.VMEM((2, QUARTER, K), jnp.float32)],
        ),
        out_shape=[jax.ShapeDtypeStruct((QUARTER, K), jnp.float32)] * 2,
        compiler_params=pltpu.CompilerParams(vmem_limit_bytes=32 * 2**20),
        cost_estimate=pl.CostEstimate(flops=2 * 2 * QUARTER * WIDTH * K, bytes_accessed=2 * QUARTER * WIDTH * 2, transcendentals=0),
        name="sketch",
    )(place, keep_mask, weights, test_matrix)


def turn_kernel(place, *refs):
    parts, out, rows = refs[:4], refs[4], refs[5]
    for m in range(4):
        rows[pl.ds(pl.multiple_of((place[1] ^ m) * SUB, 8), SUB), :] = parts[m][...]
    out[...] = rows[...].T


def turn(place, parts):
    return pl.pallas_call(
        turn_kernel,
        in_specs=[pl.BlockSpec(memory_space=pltpu.SMEM)] + [pl.BlockSpec(memory_space=pltpu.VMEM)] * 4,
        out_specs=pl.BlockSpec(memory_space=pltpu.VMEM),
        out_shape=jax.ShapeDtypeStruct((K, QUARTER), jnp.float32),
        scratch_shapes=[pltpu.VMEM((QUARTER, K), jnp.float32)],
        name="turn",
    )(place, *parts)


def gram_kernel(place, *refs):
    parts, out, whole = refs[:4], refs[4], refs[5]
    for k in range(4):
        whole[:, pl.ds(pl.multiple_of((place[0] ^ k) * QUARTER, BLOCK), QUARTER)] = parts[k][...]
    out[...] = lax.dot_general(
        whole[...], whole[...], (((1,), (1,)), ((), ())), precision=HIGHEST, preferred_element_type=jnp.float32
    )


def gram_of(place, parts):
    return pl.pallas_call(
        gram_kernel,
        in_specs=[pl.BlockSpec(memory_space=pltpu.SMEM)] + [pl.BlockSpec(memory_space=pltpu.VMEM)] * 4,
        out_specs=pl.BlockSpec(memory_space=pltpu.VMEM),
        out_shape=jax.ShapeDtypeStruct((K, K), jnp.float32),
        scratch_shapes=[pltpu.VMEM((K, ROWS), jnp.float32)],
        cost_estimate=pl.CostEstimate(flops=12 * ROWS * K * K, bytes_accessed=4 * ROWS * K, transcendentals=0),
        name="gram",
    )(place, *parts)


def inverse_factor_kernel(mine, theirs, out, step=4):
    gram = mine[...] + theirs[...]
    lanes = lax.broadcasted_iota(jnp.int32, (K, K), 1)
    rows = lax.broadcasted_iota(jnp.int32, (K, K), 0)
    unit = jnp.where(lanes == rows, 1.0, 0.0).astype(jnp.float32)
    for top in range(0, K, step):
        left = K - top
        column = [jnp.broadcast_to(gram[:, top + i : top + i + 1], (left, K)) for i in range(step)]
        row = [gram[i : i + 1, :] for i in range(step)]
        side = [unit[i : i + 1, :] for i in range(step)]
        for i in range(step):
            pivot = column[i][i : i + 1, :]
            inverse = 1.0 / pivot
            for m in range(i + 1, step):
                factor = column[i][m : m + 1, :] * inverse
                column[m] = column[m] - column[i] * factor
                row[m] = row[m] - row[i] * factor
                side[m] = side[m] - side[i] * factor
            out[top + i : top + i + 1, :] = side[i] * lax.rsqrt(pivot)
            row[i] = row[i] * inverse
            side[i] = side[i] * inverse
        if left > step:
            gram, unit = gram[step:], unit[step:]
            for i in range(step):
                gram = gram - column[i][step:] * row[i]
                unit = unit - column[i][step:] * side[i]


def inverse_factor(mine, theirs):
    return pl.pallas_call(
        inverse_factor_kernel,
        in_specs=[pl.BlockSpec(memory_space=pltpu.VMEM)] * 2,
        out_specs=pl.BlockSpec(memory_space=pltpu.VMEM),
        out_shape=jax.ShapeDtypeStruct((K, K), jnp.float32),
        cost_estimate=pl.CostEstimate(flops=10**9, bytes_accessed=2 * 10**7, transcendentals=0),
        name="inverse_factor",
    )(mine, theirs)


def projection_kernel(place, keep, first, tiles, *refs):
    parts, weights, outs, sketch = refs[:4], refs[4], refs[5:7], refs[7]
    t = pl.program_id(0)

    @pl.when(t == 0)
    def _():
        for k in range(4):
            at = pl.ds(pl.multiple_of((place[0] ^ k) * QUARTER, BLOCK), QUARTER)
            high = parts[k][...].astype(jnp.bfloat16)
            sketch[0:K, at] = high
            sketch[K : 2 * K, at] = (parts[k][...] - high.astype(jnp.float32)).astype(jnp.bfloat16)

    tile = masked(weights[...], keep, 0, first(t, place) * (TILE // BLOCK))
    both = jnp.dot(sketch[...], tile, preferred_element_type=jnp.float32)
    total = both[:K] + both[K:]
    for i, out in enumerate(outs):

        @pl.when(t // tiles == i)
        def _():
            out[...] = total


def projection_parts(place, keep_mask, weights, parts, near, offset, count):
    tiles = count // TILE

    def first(t, place):
        chip = place[2] if near else 1 - place[2]
        core = jnp.where(t < tiles, 1 - place[3], place[3])
        return (chip * 2 + core) * (WIDTH // 4 // TILE) + offset // TILE + lax.rem(t, tiles)

    return pl.pallas_call(
        lambda place, keep, *refs: projection_kernel(place, keep, first, tiles, *refs),
        grid_spec=pltpu.PrefetchScalarGridSpec(
            num_scalar_prefetch=2,
            grid=(2 * tiles,),
            in_specs=[pl.BlockSpec((K, QUARTER), lambda t, place, keep: (0, 0))] * 4
            + [pl.BlockSpec((ROWS, TILE), lambda t, place, keep: (0, first(t, place)))],
            out_specs=[
                pl.BlockSpec((K, TILE), lambda t, place, keep: (0, jnp.minimum(t, tiles - 1))),
                pl.BlockSpec((K, TILE), lambda t, place, keep: (0, jnp.maximum(t - tiles, 0))),
            ],
            scratch_shapes=[pltpu.VMEM((2 * K, ROWS), jnp.bfloat16)],
        ),
        out_shape=[jax.ShapeDtypeStruct((K, count), jnp.float32)] * 2,
        compiler_params=pltpu.CompilerParams(vmem_limit_bytes=32 * 2**20),
        cost_estimate=pl.CostEstimate(flops=8 * ROWS * K * count, bytes_accessed=4 * ROWS * count, transcendentals=0),
        name="project",
    )(place, keep_mask, *parts, weights)


def basis_kernel(place, inverse, *refs):
    parts, out = refs[:4], refs[4]
    t = pl.program_id(0)
    for k in range(4):

        @pl.when((place[0] ^ k) == t)
        def _():
            turned = jnp.dot(inverse[...], parts[k][...], precision=HIGHEST, preferred_element_type=jnp.float32)
            out[...] = (turned * math.sqrt(D)).T


def range_basis_of(place, inverse, parts):
    return pl.pallas_call(
        basis_kernel,
        grid_spec=pltpu.PrefetchScalarGridSpec(
            num_scalar_prefetch=1,
            grid=(4,),
            in_specs=[pl.BlockSpec((K, K), lambda t, place: (0, 0))]
            + [pl.BlockSpec((K, QUARTER), lambda t, place: (0, 0))] * 4,
            out_specs=pl.BlockSpec((QUARTER, K), lambda t, place: (t, 0)),
        ),
        out_shape=jax.ShapeDtypeStruct((ROWS, K), jnp.float32),
        cost_estimate=pl.CostEstimate(flops=12 * ROWS * K * K, bytes_accessed=8 * ROWS * K, transcendentals=0),
        name="basis",
    )(place, inverse, *parts)


def finish_kernel(inverse, here, core, far_a, far_b, out):
    t = pl.program_id(0)
    for i, far in enumerate((far_a, far_b)):

        @pl.when(t // 2 == i)
        def _():
            total = here[...] + core[...] + far[...]
            out[...] = jnp.dot(inverse[...], total, precision=HIGHEST, preferred_element_type=jnp.float32).T


def finish(inverse, here, core, far_a, far_b):
    half = pl.BlockSpec((K, QUARTER), lambda t: (0, t))
    return pl.pallas_call(
        finish_kernel,
        grid=(4,),
        in_specs=[
            pl.BlockSpec((K, K), lambda t: (0, 0)),
            half,
            half,
            pl.BlockSpec((K, QUARTER), lambda t: (0, jnp.minimum(t, 1))),
            pl.BlockSpec((K, QUARTER), lambda t: (0, jnp.maximum(t - 2, 0))),
        ],
        out_specs=pl.BlockSpec((QUARTER, K), lambda t: (t, 0)),
        out_shape=jax.ShapeDtypeStruct((ROWS, K), jnp.float32),
        cost_estimate=pl.CostEstimate(flops=12 * ROWS * K * K, bytes_accessed=16 * ROWS * K, transcendentals=0),
        name="finish",
    )(inverse, here, core, far_a, far_b)


def shards(weights, keep_mask, test_matrix):
    place = position()

    three = sketch_parts(2, place, keep_mask, weights, test_matrix)
    got3, got2 = swap(three[1], square(True, 3)), swap(three[0], square(True, 2))
    own = sketch_parts(0, place, keep_mask, weights, test_matrix)
    got1 = swap(own[1], square(True, 1))
    quarter = own[0] + got1 + got2 + got3
    piece = [quarter[m * SUB : (m + 1) * SUB] for m in range(4)]
    got = [swap(piece[m], square(False, m)) for m in (3, 2, 1)]
    sub = piece[0] + got[2] + got[1] + got[0]
    sub = sub + swap(sub, ACROSS)

    got = {m: swap(sub, square(False, m)) for m in (3, 2, 1)}
    mine = turn(place, (sub, got[1], got[2], got[3]))
    got = {k: swap(mine, square(True, k)) for k in (3, 2, 1)}
    parts = (mine, got[1], got[2], got[3])

    half = WIDTH // 8
    far = []
    for i in range(2):
        send, stay = projection_parts(place, keep_mask, weights, parts, False, i * half, half)
        far.append(swap(stay + swap(send, CORES), CHIPS))
    send, here = projection_parts(place, keep_mask, weights, parts, True, 0, 2 * half)
    core = swap(send, CORES)

    gram = gram_of(place, parts)
    gram = gram + swap(gram, CORES)
    inverse = inverse_factor(gram, swap(gram, CHIPS))
    return range_basis_of(place, inverse, parts), finish(inverse, here, core, *far)


def solution(mesh):
    placed = (P("rep", "shard"), P("rep", "shard"), P("shard", None))
    return jax.shard_map(
        shards,
        mesh=mesh,
        in_specs=placed,
        out_specs=(P("rep", None), P(("shard", "rep"), None)),
        check_vma=False,
    )
```

```python
import itertools
import math

import jax
import jax.numpy as jnp
from jax import lax
from jax.experimental import pallas as pl
from jax.experimental.pallas import tpu as pltpu
from jax.sharding import PartitionSpec as P

D = 6144
K = 128
BLOCK = 128
ROWS = 1536
WIDTH = 6144
QUARTER = ROWS // 4
SUB = QUARTER // 4
PANEL = 1536
PANELS = WIDTH // PANEL
TILE = 384
TILES = WIDTH // 2 // TILE
MIB = 2**20
AXES = ("shard", "rep")
HIGHEST = lax.Precision.HIGHEST
SCALARS = pl.BlockSpec(memory_space=pltpu.SMEM)
WHOLE = pl.BlockSpec(memory_space=pltpu.VMEM)
ANYWHERE = pl.BlockSpec(memory_space=pl.ANY)
SMALL = pl.CostEstimate(flops=10**6, bytes_accessed=10**5, transcendentals=0)

FOLD_A, FOLD_B = (1, 0, 3, 2), (3, 2, 1, 0)
LABEL_A, LABEL_B = (0, 1, 1, 0), (0, 0, 1, 1)


def device(z, x_hi, y, x_lo, core):
    return ((z * 2 + x_hi) * 4 + y) * 4 + x_lo * 2 + core


PLACES = list(itertools.product(range(4), range(2), range(4), range(2), range(2)))


def pairs(partner):
    return [(device(*place), device(*partner(*place))) for place in PLACES]


def square(first, bits):
    def partner(z, x_hi, y, x_lo, core):
        fold = FOLD_A if (core == 0) == first else FOLD_B
        return (fold[z] if bits & 1 else z, x_hi, fold[y] if bits & 2 else y, x_lo, core)

    return pairs(partner)


ACROSS = pairs(lambda z, x_hi, y, x_lo, core: (z, 1 - x_hi, y, x_lo, core))
CORES = pairs(lambda z, x_hi, y, x_lo, core: (z, x_hi, y, x_lo, 1 - core))
CHIPS = pairs(lambda z, x_hi, y, x_lo, core: (z, x_hi, y, 1 - x_lo, core))


def swap(value, perm):
    return lax.ppermute(value, AXES, perm)


def label(table, place):
    return sum(jnp.where(place == i, v, 0) for i, v in enumerate(table) if v)


def position():
    shard, rep = lax.axis_index("shard"), lax.axis_index("rep")
    y, z = lax.rem(shard, 4), shard // 8
    core, x_lo = lax.rem(rep, 2), rep // 2
    a = 2 * label(LABEL_A, y) + label(LABEL_A, z)
    b = 2 * label(LABEL_B, y) + label(LABEL_B, z)
    return jnp.stack([jnp.where(core == 0, a, b), jnp.where(core == 0, b, a), x_lo, core]).astype(jnp.int32)


def masked(tile, keep, row_block, col_block):
    rows, cols = tile.shape
    return jnp.concatenate(
        [
            jnp.concatenate(
                [
                    tile[r * BLOCK : (r + 1) * BLOCK, c * BLOCK : (c + 1) * BLOCK]
                    * keep[row_block + r, col_block + c].astype(jnp.float32).astype(tile.dtype)
                    for c in range(cols // BLOCK)
                ],
                axis=1,
            )
            for r in range(rows // BLOCK)
        ],
        axis=0,
    )


def sketch_kernel(place, keep, weights, test, *refs):
    outs, tiles, right, total, tile_sems, test_sems = refs[:4], *refs[4:]

    def test_copy(p):
        at = pl.ds(p * PANEL, PANEL)
        return pltpu.make_async_copy(test.at[at, :], right.at[at, :], test_sems.at[p])

    def tile_copy(p, k):
        rows = pl.ds(pl.multiple_of((place[0] ^ k) * QUARTER, QUARTER), QUARTER)
        return pltpu.make_async_copy(weights.at[rows, pl.ds(p * PANEL, PANEL)], tiles.at[p, k], tile_sems.at[p, k])

    for p in range(PANELS):
        test_copy(p).start()
        for k in range(4):
            tile_copy(p, k).start()
    for p in range(PANELS):
        test_copy(p).wait()
        for k in range(4):
            tile_copy(p, k).wait()
            tile = masked(tiles[p, k], keep, (place[0] ^ k) * (QUARTER // BLOCK), p * (PANEL // BLOCK))
            part = jnp.dot(tile, right[p * PANEL : (p + 1) * PANEL, :], preferred_element_type=jnp.float32)
            total[k] = part if p == 0 else total[k] + part
    for k in range(4):
        for m in range(4):
            start = pl.multiple_of((place[1] ^ m) * SUB, 8)
            outs[k][m * SUB : (m + 1) * SUB, :] = total[k, pl.ds(start, SUB), :]


def sketch_parts(place, keep_mask, weights, test_matrix):
    return pl.pallas_call(
        sketch_kernel,
        in_specs=[SCALARS, SCALARS, ANYWHERE, ANYWHERE],
        out_specs=[WHOLE] * 4,
        scratch_shapes=[
            pltpu.VMEM((PANELS, 4, QUARTER, PANEL), jnp.bfloat16),
            pltpu.VMEM((WIDTH, K), jnp.bfloat16),
            pltpu.VMEM((4, QUARTER, K), jnp.float32),
            pltpu.SemaphoreType.DMA((PANELS, 4)),
            pltpu.SemaphoreType.DMA((PANELS,)),
        ],
        out_shape=[jax.ShapeDtypeStruct((QUARTER, K), jnp.float32)] * 4,
        compiler_params=pltpu.CompilerParams(vmem_limit_bytes=48 * MIB),
        cost_estimate=SMALL,
        name="sketch",
    )(place, keep_mask, weights, test_matrix)


def turn_kernel(place, *refs):
    parts, out, rows = refs[:4], refs[4], refs[5]
    for m in range(4):
        rows[pl.ds(pl.multiple_of((place[1] ^ m) * SUB, 8), SUB), :] = parts[m][...]
    out[...] = rows[...].T


def turn(place, parts):
    return pl.pallas_call(
        turn_kernel,
        in_specs=[SCALARS] + [WHOLE] * 4,
        out_specs=WHOLE,
        out_shape=jax.ShapeDtypeStruct((K, QUARTER), jnp.float32),
        scratch_shapes=[pltpu.VMEM((QUARTER, K), jnp.float32)],
        compiler_params=pltpu.CompilerParams(vmem_limit_bytes=4 * MIB),
        cost_estimate=SMALL,
        name="turn",
    )(place, *parts)


def gram_kernel(*refs):
    first, second, more, out = refs[0], refs[1], refs[2:-1], refs[-1]

    def square_of(piece):
        return lax.dot_general(
            piece[...], piece[...], (((1,), (1,)), ((), ())), precision=HIGHEST, preferred_element_type=jnp.float32
        )

    total = square_of(first) + square_of(second)
    for before in more:
        total = total + before[...]
    out[...] = total


def gram_of(*parts):
    return pl.pallas_call(
        gram_kernel,
        in_specs=[WHOLE] * len(parts),
        out_specs=WHOLE,
        out_shape=jax.ShapeDtypeStruct((K, K), jnp.float32),
        compiler_params=pltpu.CompilerParams(vmem_limit_bytes=8 * MIB),
        cost_estimate=SMALL,
        name="gram",
    )(*parts)


def inverse_factor_kernel(mine, theirs, out, step=4):
    gram = mine[...] + theirs[...]
    lanes = lax.broadcasted_iota(jnp.int32, (K, K), 1)
    rows = lax.broadcasted_iota(jnp.int32, (K, K), 0)
    unit = jnp.where(lanes == rows, 1.0, 0.0).astype(jnp.float32)
    for top in range(0, K, step):
        left = K - top
        column = [jnp.broadcast_to(gram[:, top + i : top + i + 1], (left, K)) for i in range(step)]
        row = [gram[i : i + 1, :] for i in range(step)]
        side = [unit[i : i + 1, :] for i in range(step)]
        for i in range(step):
            pivot = column[i][i : i + 1, :]
            inverse = 1.0 / pivot
            for m in range(i + 1, step):
                factor = column[i][m : m + 1, :] * inverse
                column[m] = column[m] - column[i] * factor
                row[m] = row[m] - row[i] * factor
                side[m] = side[m] - side[i] * factor
            out[top + i : top + i + 1, :] = side[i] * lax.rsqrt(pivot)
            row[i] = row[i] * inverse
            side[i] = side[i] * inverse
        if left > step:
            gram, unit = gram[step:], unit[step:]
            for i in range(step):
                gram = gram - column[i][step:] * row[i]
                unit = unit - column[i][step:] * side[i]


def inverse_factor(mine, theirs):
    return pl.pallas_call(
        inverse_factor_kernel,
        in_specs=[WHOLE] * 2,
        out_specs=WHOLE,
        out_shape=jax.ShapeDtypeStruct((K, K), jnp.float32),
        compiler_params=pltpu.CompilerParams(vmem_limit_bytes=8 * MIB),
        cost_estimate=SMALL,
        name="inverse_factor",
    )(mine, theirs)


def tile_columns(place, near, t):
    core = 1 - place[3] if t < TILES // 2 else place[3]
    chip = place[2] if near else 1 - place[2]
    return (chip * 2 + core) * (WIDTH // 4 // BLOCK) + t % (TILES // 2) * (TILE // BLOCK)


def tile_copy(place, near, t, weights, tiles, sems):
    columns = pl.ds(pl.multiple_of(tile_columns(place, near, t) * BLOCK, BLOCK), TILE)
    return pltpu.make_async_copy(weights.at[:, columns], tiles.at[t], sems.at[t])


def stage_kernel(place, weights, ready, tiles, sems):
    copies = [tile_copy(place, False, t, weights, tiles, sems) for t in range(TILES)]
    for copy in copies:
        copy.start()
    for copy in copies:
        copy.wait()


def stage(place, weights, ready):
    return pl.pallas_call(
        stage_kernel,
        in_specs=[SCALARS, ANYWHERE, ANYWHERE],
        out_specs=WHOLE,
        out_shape=jax.ShapeDtypeStruct((TILES, ROWS, TILE), jnp.bfloat16),
        scratch_shapes=[pltpu.SemaphoreType.DMA((TILES,))],
        compiler_params=pltpu.CompilerParams(vmem_limit_bytes=44 * MIB),
        cost_estimate=SMALL,
        name="stage",
    )(place, weights, ready)


def project(place, keep, near, parts, write, sketch, tile):
    for k in range(4):
        at = pl.ds(pl.multiple_of((place[0] ^ k) * QUARTER, BLOCK), QUARTER)
        high = parts[k][...].astype(jnp.bfloat16)
        sketch[0:K, at] = high
        sketch[K : 2 * K, at] = (parts[k][...] - high.astype(jnp.float32)).astype(jnp.bfloat16)
    for t in range(TILES):
        both = jnp.dot(
            sketch[...], masked(tile(t), keep, 0, tile_columns(place, near, t)), preferred_element_type=jnp.float32
        )
        write(t, both[:K] + both[K:])


def far_kernel(place, keep, *refs):
    parts, tiles, outs, sketch = refs[:4], refs[4], refs[5:-1], refs[-1]

    def write(t, value):
        outs[t // (TILES // 2)][:, t % (TILES // 2) * TILE : (t % (TILES // 2) + 1) * TILE] = value

    project(place, keep, False, parts, write, sketch, lambda t: tiles[t])


def near_kernel(place, keep, *refs):
    parts, weights, outs, tiles, sketch, sems = refs[:4], refs[4], refs[5:-3], *refs[-3:]
    copies = [tile_copy(place, True, t, weights, tiles, sems) for t in range(TILES)]
    for copy in copies:
        copy.start()

    def tile(t):
        copies[t].wait()
        return tiles[t]

    def write(t, value):
        outs[t][...] = value

    project(place, keep, True, parts, write, sketch, tile)


def far_terms(place, keep_mask, parts, tiles):
    return pl.pallas_call(
        far_kernel,
        in_specs=[SCALARS, SCALARS] + [WHOLE] * 5,
        out_specs=[WHOLE] * 2,
        scratch_shapes=[pltpu.VMEM((2 * K, ROWS), jnp.bfloat16)],
        out_shape=[jax.ShapeDtypeStruct((K, WIDTH // 4), jnp.float32)] * 2,
        compiler_params=pltpu.CompilerParams(vmem_limit_bytes=32 * MIB),
        cost_estimate=SMALL,
        name="far",
    )(place, keep_mask, *parts, tiles)


def near_terms(place, keep_mask, parts, weights):
    return pl.pallas_call(
        near_kernel,
        in_specs=[SCALARS, SCALARS] + [WHOLE] * 4 + [ANYWHERE],
        out_specs=[WHOLE] * TILES,
        scratch_shapes=[
            pltpu.VMEM((TILES, ROWS, TILE), jnp.bfloat16),
            pltpu.VMEM((2 * K, ROWS), jnp.bfloat16),
            pltpu.SemaphoreType.DMA((TILES,)),
        ],
        out_shape=[jax.ShapeDtypeStruct((K, TILE), jnp.float32)] * TILES,
        compiler_params=pltpu.CompilerParams(vmem_limit_bytes=48 * MIB),
        cost_estimate=SMALL,
        name="near",
    )(place, keep_mask, *parts, weights)


def dot_split(left, right):
    def terms(x):
        high = x.astype(jnp.bfloat16)
        return high, (x - high.astype(jnp.float32)).astype(jnp.bfloat16)

    (a, b), (c, d) = terms(left), terms(right)
    return jnp.dot(
        jnp.concatenate([a, a, b], axis=1), jnp.concatenate([c, d, c], axis=0), preferred_element_type=jnp.float32
    )


def write_turned(inverse, columns, scale, out, held, sems):
    copies = []
    for t in range(4):
        value, place = columns(t)
        held[t] = (dot_split(inverse, value) * scale).T
        rows = pl.ds(pl.multiple_of(place * QUARTER, QUARTER), QUARTER)
        copies.append(pltpu.make_async_copy(held.at[t], out.at[rows, :], sems.at[t]))
        copies[-1].start()
    for copy in copies:
        copy.wait()


TURNED = dict(
    out_specs=pl.BlockSpec(memory_space=pl.ANY),
    out_shape=jax.ShapeDtypeStruct((ROWS, K), jnp.float32),
    scratch_shapes=[pltpu.VMEM((4, QUARTER, K), jnp.float32), pltpu.SemaphoreType.DMA((4,))],
    compiler_params=pltpu.CompilerParams(vmem_limit_bytes=16 * MIB),
    cost_estimate=SMALL,
)


def basis_kernel(place, inverse, *refs):
    parts, out, held, sems = refs[:4], *refs[4:]
    write_turned(inverse[...], lambda k: (parts[k][...], place[0] ^ k), math.sqrt(D), out, held, sems)


def range_basis_of(place, inverse, parts):
    return pl.pallas_call(basis_kernel, in_specs=[SCALARS] + [WHOLE] * 5, name="basis", **TURNED)(place, inverse, *parts)


def finish_kernel(inverse, far, *refs):
    terms, out, held, sems = refs[:8], *refs[8:]

    def columns(t):
        return terms[t][...] + terms[t + 4][...] + far[:, t * TILE : (t + 1) * TILE], t

    write_turned(inverse[...], columns, 1.0, out, held, sems)


def finish(inverse, far, here, core):
    return pl.pallas_call(finish_kernel, in_specs=[WHOLE] * 10, name="finish", **TURNED)(inverse, far, *here, *core)


def shards(weights, keep_mask, test_matrix):
    place = position()

    own = sketch_parts(place, keep_mask, weights, test_matrix)
    got = [swap(own[k], square(True, k)) for k in (3, 2, 1)]
    quarter = own[0] + got[2] + got[1] + got[0]
    piece = [quarter[m * SUB : (m + 1) * SUB] for m in range(4)]
    got = [swap(piece[m], square(False, m)) for m in (3, 2, 1)]
    sub = piece[0] + got[2] + got[1] + got[0]
    sub = sub + swap(sub, ACROSS)

    got = {m: swap(sub, square(False, m)) for m in (3, 2, 1)}
    mine = turn(place, (sub, got[1], got[2], got[3]))
    got = {k: swap(mine, square(True, k)) for k in (3, 2, 1)}
    parts = (mine, got[1], got[2], got[3])
    tiles = stage(place, weights, mine)

    gram = gram_of(got[2], got[3], gram_of(mine, got[1]))
    gram, parts = lax.optimization_barrier((gram, parts))
    send, stay = far_terms(place, keep_mask, parts, tiles)
    gram = gram + swap(gram, CORES)
    stay, gram = lax.optimization_barrier((stay + swap(send, CORES), gram))
    far_gram = swap(gram, CHIPS)
    far = swap(stay, CHIPS)
    terms = near_terms(place, keep_mask, parts, weights)
    core = [swap(term, CORES) for term in terms[:4]]
    inverse = inverse_factor(gram, far_gram)
    return range_basis_of(place, inverse, parts), finish(inverse, far, terms[4:], core)


def solution(mesh):
    placed = (P("rep", "shard"), P("rep", "shard"), P("shard", None))
    return jax.shard_map(
        shards,
        mesh=mesh,
        in_specs=placed,
        out_specs=(P("rep", None), P(("shard", "rep"), None)),
        check_vma=False,
    )
```

```python
import itertools
import math

import jax
import jax.numpy as jnp
from jax import lax
from jax.experimental import pallas as pl
from jax.experimental.pallas import tpu as pltpu
from jax.sharding import PartitionSpec as P

D = 6144
K = 128
BLOCK = 128
ROWS = 1536
WIDTH = 6144
QUARTER = ROWS // 4
PANEL = 1536
CHUNK = WIDTH // 8
MIB = 2**20
AXES = ("shard", "rep")
HIGHEST = lax.Precision.HIGHEST
SCALARS = pl.BlockSpec(memory_space=pltpu.SMEM)
WHOLE = pl.BlockSpec(memory_space=pltpu.VMEM)
FAR = pl.BlockSpec(memory_space=pltpu.HBM)
SMALL = pl.CostEstimate(flops=10**6, bytes_accessed=10**5, transcendentals=0)

FOLD_A, FOLD_B = (1, 0, 3, 2), (3, 2, 1, 0)
LABEL_A, LABEL_B = (0, 1, 1, 0), (0, 0, 1, 1)


def device(z, x_hi, y, x_lo, core):
    return ((z * 2 + x_hi) * 4 + y) * 4 + x_lo * 2 + core


PLACES = list(itertools.product(range(4), range(2), range(4), range(2), range(2)))


def pairs(partner):
    return [(device(*place), device(*partner(*place))) for place in PLACES]


def square(first, bits):
    def partner(z, x_hi, y, x_lo, core):
        fold = FOLD_A if (core == 0) == first else FOLD_B
        return (fold[z] if bits & 1 else z, x_hi, fold[y] if bits & 2 else y, x_lo, core)

    return pairs(partner)


ACROSS = pairs(lambda z, x_hi, y, x_lo, core: (z, 1 - x_hi, y, x_lo, core))
CORES = pairs(lambda z, x_hi, y, x_lo, core: (z, x_hi, y, x_lo, 1 - core))
CHIPS = pairs(lambda z, x_hi, y, x_lo, core: (z, x_hi, y, 1 - x_lo, core))


def swap(value, perm):
    return lax.ppermute(value, AXES, perm)


def label(table, place):
    return sum(jnp.where(place == i, v, 0) for i, v in enumerate(table) if v)


def position():
    shard, rep = lax.axis_index("shard"), lax.axis_index("rep")
    y, z = lax.rem(shard, 4), shard // 8
    core, x_lo = lax.rem(rep, 2), rep // 2
    a = 2 * label(LABEL_A, y) + label(LABEL_A, z)
    b = 2 * label(LABEL_B, y) + label(LABEL_B, z)
    return jnp.stack([jnp.where(core == 0, a, b), jnp.where(core == 0, b, a), x_lo, core]).astype(jnp.int32)


def masked(tile, keep, row_block, col_block):
    rows, cols = tile.shape
    return jnp.concatenate(
        [
            jnp.concatenate(
                [
                    tile[r * BLOCK : (r + 1) * BLOCK, c * BLOCK : (c + 1) * BLOCK]
                    * keep[row_block + r, col_block + c].astype(jnp.float32).astype(tile.dtype)
                    for c in range(cols // BLOCK)
                ],
                axis=1,
            )
            for r in range(rows // BLOCK)
        ],
        axis=0,
    )


def sketch_kernel(ks, pieces, fetch, place, keep_mask, weights, test, *refs):
    outs, refs = refs[:pieces], refs[pieces:]
    if fetch:
        right, test_sems, refs = refs[0], refs[-1], refs[1:-1]
    else:
        right = test
    keep, tiles, total, keep_sem, tile_sems = refs

    def copies(p):
        at = pl.ds(p * PANEL, PANEL)
        every = [pltpu.make_async_copy(test.at[at, :], right.at[at, :], test_sems.at[p])] if fetch else []
        for i, k in enumerate(ks):
            rows = pl.ds(pl.multiple_of((place[0] ^ k) * QUARTER, QUARTER), QUARTER)
            every.append(pltpu.make_async_copy(weights.at[rows, at], tiles.at[i, :, at], tile_sems.at[p, i]))
        return every

    keep_copy = pltpu.make_async_copy(keep_mask, keep, keep_sem)
    keep_copy.start()
    for p in range(WIDTH // PANEL):
        for copy in copies(p):
            copy.start()
    keep_copy.wait()
    height = QUARTER if len(ks) > 1 else BLOCK
    for p in range(WIDTH // PANEL):
        for copy in copies(p):
            copy.wait()
        at = slice(p * PANEL, (p + 1) * PANEL)
        for i, k in enumerate(ks):
            for r in range(0, QUARTER, height):
                rows = slice(r, r + height)
                row_block = (place[0] ^ k) * (QUARTER // BLOCK) + r // BLOCK
                tile = masked(tiles[i, rows, at], keep, row_block, p * (PANEL // BLOCK))
                part = jnp.dot(tile, right[at, :], preferred_element_type=jnp.float32)
                total[i, rows, :] = part if p == 0 else total[i, rows, :] + part
    for i, out in enumerate(outs):
        first = i * out.shape[0]
        out[...] = total[first // QUARTER, first % QUARTER : first % QUARTER + out.shape[0], :]


def sketch_parts(ks, pieces, place, keep_mask, weights, test_matrix, fetch=False):
    panels = WIDTH // PANEL
    scratch = [
        pltpu.SMEM((ROWS // BLOCK, WIDTH // BLOCK), jnp.int32),
        pltpu.VMEM((len(ks), QUARTER, WIDTH), jnp.bfloat16),
        pltpu.VMEM((len(ks), QUARTER, K), jnp.float32),
        pltpu.SemaphoreType.DMA,
        pltpu.SemaphoreType.DMA((panels, len(ks))),
    ]
    outs = [jax.ShapeDtypeStruct((QUARTER * len(ks) // pieces, K), jnp.float32)] * pieces
    if fetch:
        scratch.append(pltpu.SemaphoreType.DMA((panels,)))
        outs.append(jax.ShapeDtypeStruct((WIDTH, K), jnp.bfloat16))
    return pl.pallas_call(
        lambda *refs: sketch_kernel(ks, pieces, fetch, *refs),
        in_specs=[SCALARS, FAR, FAR, FAR if fetch else WHOLE],
        out_specs=[WHOLE] * len(outs),
        scratch_shapes=scratch,
        out_shape=outs,
        compiler_params=pltpu.CompilerParams(vmem_limit_bytes=52 * MIB),
        cost_estimate=SMALL,
        name="sketch",
    )(place, keep_mask, weights, test_matrix)


def turn_kernel(rows, out):
    out[...] = rows[...].T


def turn(quarter):
    return pl.pallas_call(
        turn_kernel,
        in_specs=[WHOLE],
        out_specs=WHOLE,
        out_shape=jax.ShapeDtypeStruct((K, QUARTER), jnp.float32),
        compiler_params=pltpu.CompilerParams(vmem_limit_bytes=4 * MIB),
        cost_estimate=SMALL,
        name="turn",
    )(quarter)


def gram_pair(first, second):
    def square_of(piece):
        return lax.dot_general(
            piece[...], piece[...], (((1,), (1,)), ((), ())), precision=HIGHEST, preferred_element_type=jnp.float32
        )

    return square_of(first) + square_of(second)


def inverse_factor_kernel(mine, theirs, out, step=4):
    gram = mine[:, CHUNK:] + theirs[:, CHUNK:]
    lanes = lax.broadcasted_iota(jnp.int32, (K, K), 1)
    rows = lax.broadcasted_iota(jnp.int32, (K, K), 0)
    unit = jnp.where(lanes == rows, 1.0, 0.0).astype(jnp.float32)
    for top in range(0, K, step):
        left = K - top
        column = [jnp.broadcast_to(gram[:, top + i : top + i + 1], (left, K)) for i in range(step)]
        row = [gram[i : i + 1, :] for i in range(step)]
        side = [unit[i : i + 1, :] for i in range(step)]
        for i in range(step):
            pivot = column[i][i : i + 1, :]
            inverse = 1.0 / pivot
            for m in range(i + 1, step):
                factor = column[i][m : m + 1, :] * inverse
                column[m] = column[m] - column[i] * factor
                row[m] = row[m] - row[i] * factor
                side[m] = side[m] - side[i] * factor
            out[top + i : top + i + 1, :] = side[i] * lax.rsqrt(pivot)
            row[i] = row[i] * inverse
            side[i] = side[i] * inverse
        if left > step:
            gram, unit = gram[step:], unit[step:]
            for i in range(step):
                gram = gram - column[i][step:] * row[i]
                unit = unit - column[i][step:] * side[i]


def inverse_factor(mine, theirs):
    return pl.pallas_call(
        inverse_factor_kernel,
        in_specs=[WHOLE] * 2,
        out_specs=WHOLE,
        out_shape=jax.ShapeDtypeStruct((K, K), jnp.float32),
        compiler_params=pltpu.CompilerParams(vmem_limit_bytes=8 * MIB),
        cost_estimate=SMALL,
        name="inverse_factor",
    )(mine, theirs)


def quarter_column(place, near, own):
    chip = place[2] if near else 1 - place[2]
    core = place[3] if own else 1 - place[3]
    return (chip * 2 + core) * (WIDTH // 4 // BLOCK)


def quarter_copies(place, near, own, weights, tile, sems):
    copies = []
    for k in range(4):
        columns = pl.ds(pl.multiple_of(quarter_column(place, near, own) * BLOCK, BLOCK), WIDTH // 4)
        rows = pl.ds(pl.multiple_of((place[0] ^ k) * QUARTER, QUARTER), QUARTER)
        at = pl.ds(k * QUARTER, QUARTER)
        copies.append(pltpu.make_async_copy(weights.at[rows, columns], tile.at[at, :], sems.at[k]))
    return copies


def kept(place, near, own, k, tile, keep):
    rows = slice(k * QUARTER, (k + 1) * QUARTER)
    return masked(tile[rows, :], keep, (place[0] ^ k) * (QUARTER // BLOCK), quarter_column(place, near, own))


def stage_kernel(own, place, keep_mask, weights, ready, out, keep, keep_sem, sems):
    keep_copy = pltpu.make_async_copy(keep_mask, keep, keep_sem)
    keep_copy.start()
    copies = quarter_copies(place, False, own, weights, out, sems)
    for copy in copies:
        copy.start()
    keep_copy.wait()
    for k in range(4):
        copies[k].wait()
        out[k * QUARTER : (k + 1) * QUARTER, :] = kept(place, False, own, k, out, keep)


def stage(own, place, keep_mask, weights, ready):
    return pl.pallas_call(
        lambda *refs: stage_kernel(own, *refs),
        in_specs=[SCALARS, FAR, FAR, FAR],
        out_specs=WHOLE,
        out_shape=jax.ShapeDtypeStruct((ROWS, WIDTH // 4), jnp.bfloat16),
        scratch_shapes=[
            pltpu.SMEM((ROWS // BLOCK, WIDTH // BLOCK), jnp.int32),
            pltpu.SemaphoreType.DMA,
            pltpu.SemaphoreType.DMA((4,)),
        ],
        compiler_params=pltpu.CompilerParams(vmem_limit_bytes=46 * MIB),
        cost_estimate=SMALL,
        name="stage",
    )(place, keep_mask, weights, ready)


def two_terms(first, second, sketch):
    for k, part in enumerate((first, second)):
        at = slice(k * QUARTER, (k + 1) * QUARTER)
        high = part[...].astype(jnp.bfloat16)
        sketch[0:K, at] = high
        sketch[K : 2 * K, at] = (part[...] - high.astype(jnp.float32)).astype(jnp.bfloat16)


def project(sketch, tile):
    both = jnp.dot(sketch[...], tile, preferred_element_type=jnp.float32)
    return both[:K] + both[K:]


def begin_kernel(first, second, send_tile, stay_tile, gram, sketch, send, stay):
    two_terms(first, second, sketch)
    gram[...] = gram_pair(first, second)
    send[...] = project(sketch, send_tile[: 2 * QUARTER, :])
    stay[...] = project(sketch, stay_tile[: 2 * QUARTER, :])


def begin(first, second, send_tile, stay_tile):
    return pl.pallas_call(
        begin_kernel,
        in_specs=[WHOLE] * 4,
        out_specs=[WHOLE] * 4,
        out_shape=[
            jax.ShapeDtypeStruct((K, K), jnp.float32),
            jax.ShapeDtypeStruct((2 * K, 2 * QUARTER), jnp.bfloat16),
            jax.ShapeDtypeStruct((K, WIDTH // 4), jnp.float32),
            jax.ShapeDtypeStruct((K, WIDTH // 4), jnp.float32),
        ],
        compiler_params=pltpu.CompilerParams(vmem_limit_bytes=16 * MIB),
        cost_estimate=SMALL,
        name="begin",
    )(first, second, send_tile, stay_tile)


def first_kernel(first, second, gram, tile, before, out, sketch):
    two_terms(first, second, sketch)
    out[:, :CHUNK] = before[:, :CHUNK] + project(sketch, tile[2 * QUARTER :, :CHUNK])
    out[:, CHUNK:] = gram[...] + gram_pair(first, second)


def first_term(first, second, gram, tile, before):
    return pl.pallas_call(
        first_kernel,
        in_specs=[WHOLE] * 5,
        out_specs=[WHOLE] * 2,
        out_shape=[
            jax.ShapeDtypeStruct((K, CHUNK + K), jnp.float32),
            jax.ShapeDtypeStruct((2 * K, 2 * QUARTER), jnp.bfloat16),
        ],
        compiler_params=pltpu.CompilerParams(vmem_limit_bytes=16 * MIB),
        cost_estimate=SMALL,
        name="first",
    )(first, second, gram, tile, before)


def far_kernel(start, sketch, tile, before, out):
    at = slice(start, start + CHUNK)
    out[...] = before[:, at] + project(sketch, tile[2 * QUARTER :, at])


def far_term(start, sketch, tile, before):
    return pl.pallas_call(
        lambda *refs: far_kernel(start, *refs),
        in_specs=[WHOLE] * 3,
        out_specs=WHOLE,
        out_shape=jax.ShapeDtypeStruct((K, CHUNK), jnp.float32),
        compiler_params=pltpu.CompilerParams(vmem_limit_bytes=16 * MIB),
        cost_estimate=SMALL,
        name="far",
    )(sketch, tile, before)


def near_kernel(place, keep_mask, sketch_a, sketch_b, weights, *refs):
    outs, keep, tiles, keep_sem, sems = refs[:8], *refs[8:]
    keep_copy = pltpu.make_async_copy(keep_mask, keep, keep_sem)
    keep_copy.start()
    copies = [quarter_copies(place, True, i == 1, weights, tiles.at[i], sems.at[i]) for i in range(2)]
    for copy in copies[0] + copies[1]:
        copy.start()
    keep_copy.wait()
    for i in range(2):
        total = 0.0
        for k, sketch in enumerate((sketch_a, sketch_a, sketch_b, sketch_b)):
            copies[i][k].wait()
            at = slice(k % 2 * QUARTER, (k % 2 + 1) * QUARTER)
            total = total + project(sketch.at[:, at], kept(place, True, i == 1, k, tiles.at[i], keep))
        for t in range(4):
            outs[4 * i + t][...] = total[:, t * QUARTER : (t + 1) * QUARTER]


def near_terms(place, keep_mask, sketch_a, sketch_b, weights):
    return pl.pallas_call(
        near_kernel,
        in_specs=[SCALARS, FAR, WHOLE, WHOLE, FAR],
        out_specs=[WHOLE] * 8,
        scratch_shapes=[
            pltpu.SMEM((ROWS // BLOCK, WIDTH // BLOCK), jnp.int32),
            pltpu.VMEM((2, ROWS, WIDTH // 4), jnp.bfloat16),
            pltpu.SemaphoreType.DMA,
            pltpu.SemaphoreType.DMA((2, 4)),
        ],
        out_shape=[jax.ShapeDtypeStruct((K, QUARTER), jnp.float32)] * 8,
        compiler_params=pltpu.CompilerParams(vmem_limit_bytes=40 * MIB),
        cost_estimate=SMALL,
        name="near",
    )(place, keep_mask, sketch_a, sketch_b, weights)


def dot_split(left, right):
    def terms(x):
        high = x.astype(jnp.bfloat16)
        return high, (x - high.astype(jnp.float32)).astype(jnp.bfloat16)

    (a, b), (c, d) = terms(left), terms(right)
    return jnp.dot(
        jnp.concatenate([a, a, b], axis=1), jnp.concatenate([c, d, c], axis=0), preferred_element_type=jnp.float32
    )


def write_turned(inverse, columns, scale, out, held, sems):
    copies = []
    for t in range(4):
        value, place = columns(t)
        held[t] = (dot_split(inverse, value) * scale).T
        rows = pl.ds(pl.multiple_of(place * QUARTER, QUARTER), QUARTER)
        copies.append(pltpu.make_async_copy(held.at[t], out.at[rows, :], sems.at[t]))
        copies[-1].start()
    for copy in copies:
        copy.wait()


TURNED = dict(
    out_specs=FAR,
    out_shape=jax.ShapeDtypeStruct((ROWS, K), jnp.float32),
    scratch_shapes=[pltpu.VMEM((4, QUARTER, K), jnp.float32), pltpu.SemaphoreType.DMA((4,))],
    compiler_params=pltpu.CompilerParams(vmem_limit_bytes=16 * MIB),
    cost_estimate=SMALL,
)


def basis_kernel(place, inverse, *refs):
    parts, out, held, sems = refs[:4], *refs[4:]
    write_turned(inverse[...], lambda k: (parts[k][...], place[0] ^ k), math.sqrt(D), out, held, sems)


def range_basis_of(place, inverse, parts):
    return pl.pallas_call(basis_kernel, in_specs=[SCALARS] + [WHOLE] * 5, name="basis", **TURNED)(place, inverse, *parts)


def finish_kernel(inverse, far_a, far_b, *refs):
    terms, out, held, sems = refs[:8], *refs[8:]

    def columns(t):
        far = (far_a, far_b)[t * QUARTER // CHUNK]
        start = t * QUARTER % CHUNK
        return terms[t][...] + terms[t + 4][...] + far[:, start : start + QUARTER], t

    write_turned(inverse[...], columns, 1.0, out, held, sems)


def finish(inverse, far, here, core):
    return pl.pallas_call(finish_kernel, in_specs=[WHOLE] * 11, name="finish", **TURNED)(inverse, *far, *here, *core)


def shards(weights, keep_mask, test_matrix):
    place = position()

    two, three, test_matrix = sketch_parts((2, 3), 2, place, keep_mask, weights, test_matrix, fetch=True)
    two, three = swap(two, square(True, 2)), swap(three, square(True, 3))
    one = [swap(piece, square(True, 1)) for piece in sketch_parts((1,), 2, place, keep_mask, weights, test_matrix)]
    part = sketch_parts((0,), 1, place, keep_mask, weights, test_matrix)[0] + three + two + jnp.concatenate(one)
    part = part + swap(part, square(False, 2))
    sent = swap(part, square(False, 1))
    send_tile = stage(False, place, keep_mask, weights, part)
    part, send_tile = lax.optimization_barrier((part + sent, send_tile))
    sent = swap(part, ACROSS)
    stay_tile = stage(True, place, keep_mask, weights, part)
    part, stay_tile = lax.optimization_barrier((part + sent, stay_tile))

    mine = turn(part)
    one, two, three = (swap(mine, square(True, k)) for k in (1, 2, 3))

    gram, sketch_a, send_a, stay_a = begin(mine, one, send_tile, stay_tile)
    send, sketch_b = first_term(two, three, gram, send_tile, send_a)
    stay = jnp.concatenate([far_term(0, sketch_b, stay_tile, stay_a), send[:, CHUNK:]], axis=1)
    total = stay + swap(send, CORES)
    far_a = swap(total, CHIPS)
    send = far_term(CHUNK, sketch_b, send_tile, send_a)
    rest = far_term(CHUNK, sketch_b, stay_tile, stay_a) + swap(send, CORES)
    rest, sketch_b = lax.optimization_barrier((rest, sketch_b))
    far_b = swap(rest, CHIPS)
    terms = near_terms(place, keep_mask, sketch_a, sketch_b, weights)
    core = [swap(term, CORES) for term in terms[:4]]
    inverse = inverse_factor(total, far_a)
    basis = range_basis_of(place, inverse, (mine, one, two, three))
    return basis, finish(inverse, (far_a, far_b), terms[4:], core)


def solution(mesh):
    placed = (P("rep", "shard"), P("rep", "shard"), P("shard", None))
    return jax.shard_map(
        shards,
        mesh=mesh,
        in_specs=placed,
        out_specs=(P("rep", None), P(("shard", "rep"), None)),
        check_vma=False,
    )
```

```python
import itertools
import math

import jax
import jax.numpy as jnp
from jax import lax
from jax.experimental import pallas as pl
from jax.experimental.pallas import tpu as pltpu
from jax.sharding import PartitionSpec as P

D = 6144
K = 128
BLOCK = 128
ROWS = 1536
WIDTH = 6144
QUARTER = ROWS // 4
PANEL = 1536
CHUNK = WIDTH // 8
ORDER = (0, 3, 1, 2)
MIB = 2**20
AXES = ("shard", "rep")
HIGHEST = lax.Precision.HIGHEST
SCALARS = pl.BlockSpec(memory_space=pltpu.SMEM)
WHOLE = pl.BlockSpec(memory_space=pltpu.VMEM)
FAR = pl.BlockSpec(memory_space=pltpu.HBM)
SMALL = pl.CostEstimate(flops=10**6, bytes_accessed=10**5, transcendentals=0)

FOLD_A, FOLD_B = (1, 0, 3, 2), (3, 2, 1, 0)
LABEL_A, LABEL_B = (0, 1, 1, 0), (0, 0, 1, 1)


def device(z, x_hi, y, x_lo, core):
    return ((z * 2 + x_hi) * 4 + y) * 4 + x_lo * 2 + core


PLACES = list(itertools.product(range(4), range(2), range(4), range(2), range(2)))


def pairs(partner):
    return [(device(*place), device(*partner(*place))) for place in PLACES]


def folds(first, core):
    return (FOLD_A, FOLD_A) if (core == 0) == first else (FOLD_B, FOLD_B)


def square(first, bits):
    def partner(z, x_hi, y, x_lo, core):
        fold_y, fold_z = folds(first, core)
        return (fold_z[z] if bits & 1 else z, x_hi, fold_y[y] if bits & 2 else y, x_lo, core)

    return pairs(partner)


ACROSS = pairs(lambda z, x_hi, y, x_lo, core: (z, 1 - x_hi, y, x_lo, core))
CORES = pairs(lambda z, x_hi, y, x_lo, core: (z, x_hi, y, x_lo, 1 - core))
CHIPS = pairs(lambda z, x_hi, y, x_lo, core: (z, x_hi, y, 1 - x_lo, core))


def swap(value, perm):
    return lax.ppermute(value, AXES, perm)


def label(table, place):
    return sum(jnp.where(place == i, v, 0) for i, v in enumerate(table) if v)


def position():
    shard, rep = lax.axis_index("shard"), lax.axis_index("rep")
    y, z = lax.rem(shard, 4), shard // 8
    core, x_lo = lax.rem(rep, 2), rep // 2
    even = 2 * label(LABEL_A, y) + label(LABEL_A, z)
    odd = 2 * label(LABEL_B, y) + label(LABEL_B, z)
    return jnp.stack([jnp.where(core == 0, even, odd), x_lo, core]).astype(jnp.int32)


def masked(tile, keep, row_block, col_block):
    rows, cols = tile.shape
    return jnp.concatenate(
        [
            jnp.concatenate(
                [
                    tile[r * BLOCK : (r + 1) * BLOCK, c * BLOCK : (c + 1) * BLOCK]
                    * keep[row_block + r, col_block + c].astype(jnp.float32).astype(tile.dtype)
                    for c in range(cols // BLOCK)
                ],
                axis=1,
            )
            for r in range(rows // BLOCK)
        ],
        axis=0,
    )


def sketch_kernel(ks, place, keep_mask, weights, right, *refs):
    outs, keep, tiles, total, keep_sem, tile_sems = refs[: len(ks)], *refs[len(ks) :]

    def copies(p):
        at = pl.ds(p * PANEL, PANEL)
        every = []
        for i, k in enumerate(ks):
            rows = pl.ds(pl.multiple_of((place[0] ^ k) * QUARTER, QUARTER), QUARTER)
            every.append(pltpu.make_async_copy(weights.at[rows, at], tiles.at[i, :, at], tile_sems.at[p, i]))
        return every

    keep_copy = pltpu.make_async_copy(keep_mask, keep, keep_sem)
    keep_copy.start()
    for p in range(WIDTH // PANEL):
        for copy in copies(p):
            copy.start()
    keep_copy.wait()
    for p in range(WIDTH // PANEL):
        for copy in copies(p):
            copy.wait()
        at = slice(p * PANEL, (p + 1) * PANEL)
        for i, k in enumerate(ks):
            for r in range(0, QUARTER, BLOCK):
                rows = slice(r, r + BLOCK)
                row_block = (place[0] ^ k) * (QUARTER // BLOCK) + r // BLOCK
                tile = masked(tiles[i, rows, at], keep, row_block, p * (PANEL // BLOCK))
                part = jnp.dot(tile, right[at, :], preferred_element_type=jnp.float32)
                total[i, rows, :] = part if p == 0 else total[i, rows, :] + part
    for i, out in enumerate(outs):
        out[...] = total[i]


def sketch_parts(ks, place, keep_mask, weights, test_matrix):
    panels = WIDTH // PANEL
    scratch = [
        pltpu.SMEM((ROWS // BLOCK, WIDTH // BLOCK), jnp.int32),
        pltpu.VMEM((len(ks), QUARTER, WIDTH), jnp.bfloat16),
        pltpu.VMEM((len(ks), QUARTER, K), jnp.float32),
        pltpu.SemaphoreType.DMA,
        pltpu.SemaphoreType.DMA((panels, len(ks))),
    ]
    outs = [jax.ShapeDtypeStruct((QUARTER, K), jnp.float32)] * len(ks)
    return pl.pallas_call(
        lambda *refs: sketch_kernel(ks, *refs),
        in_specs=[SCALARS, FAR, FAR, WHOLE],
        out_specs=[WHOLE] * len(outs),
        scratch_shapes=scratch,
        out_shape=outs,
        compiler_params=pltpu.CompilerParams(vmem_limit_bytes=51 * MIB),
        cost_estimate=SMALL,
        name="sketch",
    )(place, keep_mask, weights, test_matrix)


def turn_kernel(rows, out):
    out[...] = rows[...].T


def turn(quarter):
    return pl.pallas_call(
        turn_kernel,
        in_specs=[WHOLE],
        out_specs=WHOLE,
        out_shape=jax.ShapeDtypeStruct((K, QUARTER), jnp.float32),
        compiler_params=pltpu.CompilerParams(vmem_limit_bytes=4 * MIB),
        cost_estimate=SMALL,
        name="turn",
    )(quarter)


def gram_pair(first, second):
    def square_of(piece):
        return lax.dot_general(
            piece[...], piece[...], (((1,), (1,)), ((), ())), precision=HIGHEST, preferred_element_type=jnp.float32
        )

    return square_of(first) + square_of(second)


def inverse_factor_kernel(mine, theirs, out, step=4):
    gram = mine[:, CHUNK:] + theirs[:, CHUNK:]
    lanes = lax.broadcasted_iota(jnp.int32, (K, K), 1)
    rows = lax.broadcasted_iota(jnp.int32, (K, K), 0)
    unit = jnp.where(lanes == rows, 1.0, 0.0).astype(jnp.float32)
    for top in range(0, K, step):
        left = K - top
        column = [jnp.broadcast_to(gram[:, top + i : top + i + 1], (left, K)) for i in range(step)]
        row = [gram[i : i + 1, :] for i in range(step)]
        side = [unit[i : i + 1, :] for i in range(step)]
        for i in range(step):
            pivot = column[i][i : i + 1, :]
            inverse = 1.0 / pivot
            for m in range(i + 1, step):
                factor = column[i][m : m + 1, :] * inverse
                column[m] = column[m] - column[i] * factor
                row[m] = row[m] - row[i] * factor
                side[m] = side[m] - side[i] * factor
            out[top + i : top + i + 1, :] = side[i] * lax.rsqrt(pivot)
            row[i] = row[i] * inverse
            side[i] = side[i] * inverse
        if left > step:
            gram, unit = gram[step:], unit[step:]
            for i in range(step):
                gram = gram - column[i][step:] * row[i]
                unit = unit - column[i][step:] * side[i]


def inverse_factor(mine, theirs):
    return pl.pallas_call(
        inverse_factor_kernel,
        in_specs=[WHOLE] * 2,
        out_specs=WHOLE,
        out_shape=jax.ShapeDtypeStruct((K, K), jnp.float32),
        compiler_params=pltpu.CompilerParams(vmem_limit_bytes=8 * MIB),
        cost_estimate=SMALL,
        name="inverse_factor",
    )(mine, theirs)


def quarter_column(place, near, own):
    chip = place[1] if near else 1 - place[1]
    core = place[2] if own else 1 - place[2]
    return (chip * 2 + core) * (WIDTH // 4 // BLOCK)


def quarter_copies(place, near, own, weights, tile, sems):
    copies = []
    for k in range(4):
        columns = pl.ds(pl.multiple_of(quarter_column(place, near, own) * BLOCK, BLOCK), WIDTH // 4)
        rows = pl.ds(pl.multiple_of((place[0] ^ ORDER[k]) * QUARTER, QUARTER), QUARTER)
        at = pl.ds(k * QUARTER, QUARTER)
        copies.append(pltpu.make_async_copy(weights.at[rows, columns], tile.at[at, :], sems.at[k]))
    return copies


def kept(place, near, own, k, tile, keep):
    rows = slice(k * QUARTER, (k + 1) * QUARTER)
    return masked(tile[rows, :], keep, (place[0] ^ ORDER[k]) * (QUARTER // BLOCK), quarter_column(place, near, own))


def stage_kernel(own, place, keep_mask, weights, ready, out, keep, keep_sem, sems):
    keep_copy = pltpu.make_async_copy(keep_mask, keep, keep_sem)
    keep_copy.start()
    copies = quarter_copies(place, False, own, weights, out, sems)
    for copy in copies:
        copy.start()
    keep_copy.wait()
    for k in range(4):
        copies[k].wait()
        out[k * QUARTER : (k + 1) * QUARTER, :] = kept(place, False, own, k, out, keep)


def stage(own, place, keep_mask, weights, ready):
    return pl.pallas_call(
        lambda *refs: stage_kernel(own, *refs),
        in_specs=[SCALARS, FAR, FAR, FAR],
        out_specs=WHOLE,
        out_shape=jax.ShapeDtypeStruct((ROWS, WIDTH // 4), jnp.bfloat16),
        scratch_shapes=[
            pltpu.SMEM((ROWS // BLOCK, WIDTH // BLOCK), jnp.int32),
            pltpu.SemaphoreType.DMA,
            pltpu.SemaphoreType.DMA((4,)),
        ],
        compiler_params=pltpu.CompilerParams(vmem_limit_bytes=46 * MIB),
        cost_estimate=SMALL,
        name="stage",
    )(place, keep_mask, weights, ready)


def two_terms(parts, sketch):
    for k, part in enumerate(parts):
        at = slice(k * QUARTER, (k + 1) * QUARTER)
        high = part[...].astype(jnp.bfloat16)
        sketch[0:K, at] = high
        sketch[K : 2 * K, at] = (part[...] - high.astype(jnp.float32)).astype(jnp.bfloat16)


def project(sketch, tile):
    both = jnp.dot(sketch[...], tile, preferred_element_type=jnp.float32)
    return both[:K] + both[K:]


def begin_kernel(mine, three, send_tile, stay_tile, gram, sketch, send, stay):
    two_terms((mine, three), sketch)
    gram[...] = gram_pair(mine, three)
    send[...] = project(sketch, send_tile[: 2 * QUARTER, :])
    stay[...] = project(sketch, stay_tile[: 2 * QUARTER, :])


def begin(mine, three, send_tile, stay_tile):
    return pl.pallas_call(
        begin_kernel,
        in_specs=[WHOLE] * 4,
        out_specs=[WHOLE] * 4,
        out_shape=[
            jax.ShapeDtypeStruct((K, K), jnp.float32),
            jax.ShapeDtypeStruct((2 * K, 2 * QUARTER), jnp.bfloat16),
            jax.ShapeDtypeStruct((K, WIDTH // 4), jnp.float32),
            jax.ShapeDtypeStruct((K, WIDTH // 4), jnp.float32),
        ],
        compiler_params=pltpu.CompilerParams(vmem_limit_bytes=16 * MIB),
        cost_estimate=SMALL,
        name="begin",
    )(mine, three, send_tile, stay_tile)


def first_kernel(one, two, gram, tile, before, out, sketch):
    two_terms((one, two), sketch)
    out[:, :CHUNK] = before[:, :CHUNK] + project(sketch, tile[2 * QUARTER :, :CHUNK])
    out[:, CHUNK:] = gram[...] + gram_pair(one, two)


def first_term(one, two, gram, tile, before):
    return pl.pallas_call(
        first_kernel,
        in_specs=[WHOLE] * 5,
        out_specs=[WHOLE] * 2,
        out_shape=[
            jax.ShapeDtypeStruct((K, CHUNK + K), jnp.float32),
            jax.ShapeDtypeStruct((2 * K, 2 * QUARTER), jnp.bfloat16),
        ],
        compiler_params=pltpu.CompilerParams(vmem_limit_bytes=16 * MIB),
        cost_estimate=SMALL,
        name="first",
    )(one, two, gram, tile, before)


def far_kernel(start, sketch, tile, before, out):
    at = slice(start, start + CHUNK)
    out[...] = before[:, at] + project(sketch, tile[2 * QUARTER :, at])


def far_term(start, sketch, tile, before):
    return pl.pallas_call(
        lambda *refs: far_kernel(start, *refs),
        in_specs=[WHOLE] * 3,
        out_specs=WHOLE,
        out_shape=jax.ShapeDtypeStruct((K, CHUNK), jnp.float32),
        compiler_params=pltpu.CompilerParams(vmem_limit_bytes=16 * MIB),
        cost_estimate=SMALL,
        name="far",
    )(sketch, tile, before)


def near_kernel(place, keep_mask, sketch_a, sketch_b, weights, *refs):
    outs, keep, tiles, keep_sem, sems = refs[:8], *refs[8:]
    keep_copy = pltpu.make_async_copy(keep_mask, keep, keep_sem)
    keep_copy.start()
    copies = [quarter_copies(place, True, i == 1, weights, tiles.at[i], sems.at[i]) for i in range(2)]
    for copy in copies[0] + copies[1]:
        copy.start()
    keep_copy.wait()
    for i in range(2):
        total = 0.0
        for k in range(4):
            copies[i][k].wait()
            sketch = (sketch_a, sketch_b)[k // 2].at[:, k % 2 * QUARTER : (k % 2 + 1) * QUARTER]
            total = total + project(sketch, kept(place, True, i == 1, k, tiles.at[i], keep))
        for t in range(4):
            outs[4 * i + t][...] = total[:, t * QUARTER : (t + 1) * QUARTER]


def near_terms(place, keep_mask, sketch_a, sketch_b, weights):
    return pl.pallas_call(
        near_kernel,
        in_specs=[SCALARS, FAR, WHOLE, WHOLE, FAR],
        out_specs=[WHOLE] * 8,
        scratch_shapes=[
            pltpu.SMEM((ROWS // BLOCK, WIDTH // BLOCK), jnp.int32),
            pltpu.VMEM((2, ROWS, WIDTH // 4), jnp.bfloat16),
            pltpu.SemaphoreType.DMA,
            pltpu.SemaphoreType.DMA((2, 4)),
        ],
        out_shape=[jax.ShapeDtypeStruct((K, QUARTER), jnp.float32)] * 8,
        compiler_params=pltpu.CompilerParams(vmem_limit_bytes=40 * MIB),
        cost_estimate=SMALL,
        name="near",
    )(place, keep_mask, sketch_a, sketch_b, weights)


def dot_split(left, right):
    def terms(x):
        high = x.astype(jnp.bfloat16)
        return high, (x - high.astype(jnp.float32)).astype(jnp.bfloat16)

    (a, b), (c, d) = terms(left), terms(right)
    return jnp.dot(
        jnp.concatenate([a, a, b], axis=1), jnp.concatenate([c, d, c], axis=0), preferred_element_type=jnp.float32
    )


def write_turned(inverse, columns, scale, out, held, sems):
    copies = []
    for t in range(4):
        value, place = columns(t)
        held[t] = (dot_split(inverse, value) * scale).T
        rows = pl.ds(pl.multiple_of(place * QUARTER, QUARTER), QUARTER)
        copies.append(pltpu.make_async_copy(held.at[t], out.at[rows, :], sems.at[t]))
        copies[-1].start()
    for copy in copies:
        copy.wait()


TURNED = dict(
    out_specs=FAR,
    out_shape=jax.ShapeDtypeStruct((ROWS, K), jnp.float32),
    scratch_shapes=[pltpu.VMEM((4, QUARTER, K), jnp.float32), pltpu.SemaphoreType.DMA((4,))],
    compiler_params=pltpu.CompilerParams(vmem_limit_bytes=16 * MIB),
    cost_estimate=SMALL,
)


def basis_kernel(place, inverse, *refs):
    parts, out, held, sems = refs[:4], *refs[4:]
    write_turned(inverse[...], lambda k: (parts[k][...], place[0] ^ k), math.sqrt(D), out, held, sems)


def range_basis_of(place, inverse, parts):
    return pl.pallas_call(basis_kernel, in_specs=[SCALARS] + [WHOLE] * 5, name="basis", **TURNED)(place, inverse, *parts)


def finish_kernel(inverse, far_a, far_b, *refs):
    terms, out, held, sems = refs[:8], *refs[8:]

    def columns(t):
        far = (far_a, far_b)[t * QUARTER // CHUNK]
        start = t * QUARTER % CHUNK
        return terms[t][...] + terms[t + 4][...] + far[:, start : start + QUARTER], t

    write_turned(inverse[...], columns, 1.0, out, held, sems)


def finish(inverse, far, here, core):
    return pl.pallas_call(finish_kernel, in_specs=[WHOLE] * 11, name="finish", **TURNED)(inverse, *far, *here, *core)


def shards(weights, keep_mask, test_matrix):
    place = position()

    one, two, three = sketch_parts((1, 2, 3), place, keep_mask, weights, test_matrix)
    three, two, one = swap(three, square(True, 3)), swap(two, square(True, 2)), swap(one, square(True, 1))
    part = sketch_parts((0,), place, keep_mask, weights, test_matrix)[0] + three + two + one
    one, two, three = (swap(part, square(False, k)) for k in (1, 2, 3))
    send_tile = stage(False, place, keep_mask, weights, part)
    part, send_tile = lax.optimization_barrier(((part + two) + (one + three), send_tile))
    sent = swap(part, ACROSS)
    stay_tile = stage(True, place, keep_mask, weights, part)
    part, stay_tile = lax.optimization_barrier((part + sent, stay_tile))

    mine = turn(part)
    one, two, three = (swap(mine, square(True, k)) for k in (1, 2, 3))

    gram, sketch_a, send_a, stay_a = begin(mine, three, send_tile, stay_tile)
    send, sketch_b = first_term(one, two, gram, send_tile, send_a)
    stay = jnp.concatenate([far_term(0, sketch_b, stay_tile, stay_a), send[:, CHUNK:]], axis=1)
    total = stay + swap(send, CORES)
    far_a = swap(total, CHIPS)
    send = far_term(CHUNK, sketch_b, send_tile, send_a)
    rest = far_term(CHUNK, sketch_b, stay_tile, stay_a) + swap(send, CORES)
    rest, sketch_b = lax.optimization_barrier((rest, sketch_b))
    far_b = swap(rest, CHIPS)
    terms = near_terms(place, keep_mask, sketch_a, sketch_b, weights)
    core = [swap(term, CORES) for term in terms[:4]]
    inverse = inverse_factor(total, far_a)
    basis = range_basis_of(place, inverse, (mine, one, two, three))
    return basis, finish(inverse, (far_a, far_b), terms[4:], core)


def solution(mesh):
    placed = (P("rep", "shard"), P("rep", "shard"), P("shard", None))
    return jax.shard_map(
        shards,
        mesh=mesh,
        in_specs=placed,
        out_specs=(P("rep", None), P(("shard", "rep"), None)),
        check_vma=False,
    )
```

```python
import itertools
import math

import jax
import jax.numpy as jnp
from jax import lax
from jax.experimental import pallas as pl
from jax.experimental.pallas import tpu as pltpu
from jax.sharding import PartitionSpec as P

D = 6144
K = 128
BLOCK = 128
ROWS = 1536
WIDTH = 6144
QUARTER = ROWS // 4
PANEL = 1536
CHUNK = 896
ORDER = (0, 3, 1, 2)
MIB = 2**20
AXES = ("shard", "rep")
HIGHEST = lax.Precision.HIGHEST
SCALARS = pl.BlockSpec(memory_space=pltpu.SMEM)
WHOLE = pl.BlockSpec(memory_space=pltpu.VMEM)
FAR = pl.BlockSpec(memory_space=pltpu.HBM)
SMALL = pl.CostEstimate(flops=10**6, bytes_accessed=10**5, transcendentals=0)

FOLD_A, FOLD_B = (1, 0, 3, 2), (3, 2, 1, 0)
LABEL_A, LABEL_B = (0, 1, 1, 0), (0, 0, 1, 1)


def device(z, x_hi, y, x_lo, core):
    return ((z * 2 + x_hi) * 4 + y) * 4 + x_lo * 2 + core


PLACES = list(itertools.product(range(4), range(2), range(4), range(2), range(2)))


def pairs(partner):
    return [(device(*place), device(*partner(*place))) for place in PLACES]


def folds(first, core):
    return (FOLD_A, FOLD_A) if (core == 0) == first else (FOLD_B, FOLD_B)


def square(first, bits):
    def partner(z, x_hi, y, x_lo, core):
        fold_y, fold_z = folds(first, core)
        return (fold_z[z] if bits & 1 else z, x_hi, fold_y[y] if bits & 2 else y, x_lo, core)

    return pairs(partner)


ACROSS = pairs(lambda z, x_hi, y, x_lo, core: (z, 1 - x_hi, y, x_lo, core))
CORES = pairs(lambda z, x_hi, y, x_lo, core: (z, x_hi, y, x_lo, 1 - core))
OTHERS = pairs(lambda z, x_hi, y, x_lo, core: (z, 1 - x_hi, y, 1 - x_lo, core))
CHIPS = pairs(lambda z, x_hi, y, x_lo, core: (z, x_hi, y, 1 - x_lo, core))


def swap(value, perm):
    return lax.ppermute(value, AXES, perm)


def label(table, place):
    return sum(jnp.where(place == i, v, 0) for i, v in enumerate(table) if v)


def position():
    shard, rep = lax.axis_index("shard"), lax.axis_index("rep")
    y, z = lax.rem(shard, 4), shard // 8
    core, x_lo = lax.rem(rep, 2), rep // 2
    even = 2 * label(LABEL_A, y) + label(LABEL_A, z)
    odd = 2 * label(LABEL_B, y) + label(LABEL_B, z)
    return jnp.stack([jnp.where(core == 0, even, odd), x_lo, core]).astype(jnp.int32)


def masked(tile, keep, row_block, col_block):
    rows, cols = tile.shape
    return jnp.concatenate(
        [
            jnp.concatenate(
                [
                    tile[r * BLOCK : (r + 1) * BLOCK, c * BLOCK : (c + 1) * BLOCK]
                    * keep[row_block + r, col_block + c].astype(jnp.float32).astype(tile.dtype)
                    for c in range(cols // BLOCK)
                ],
                axis=1,
            )
            for r in range(rows // BLOCK)
        ],
        axis=0,
    )


def sketch_kernel(ks, place, keep_mask, weights, right, *refs):
    outs, keep, tiles, total, keep_sem, tile_sems = refs[: len(ks)], *refs[len(ks) :]

    def copies(p):
        at = pl.ds(p * PANEL, PANEL)
        every = []
        for i, k in enumerate(ks):
            rows = pl.ds(pl.multiple_of((place[0] ^ k) * QUARTER, QUARTER), QUARTER)
            every.append(pltpu.make_async_copy(weights.at[rows, at], tiles.at[i, :, at], tile_sems.at[p, i]))
        return every

    keep_copy = pltpu.make_async_copy(keep_mask, keep, keep_sem)
    keep_copy.start()
    for p in range(WIDTH // PANEL):
        for copy in copies(p):
            copy.start()
    keep_copy.wait()
    for p in range(WIDTH // PANEL):
        for copy in copies(p):
            copy.wait()
        at = slice(p * PANEL, (p + 1) * PANEL)
        for i, k in enumerate(ks):
            for r in range(0, QUARTER, BLOCK):
                rows = slice(r, r + BLOCK)
                row_block = (place[0] ^ k) * (QUARTER // BLOCK) + r // BLOCK
                tile = masked(tiles[i, rows, at], keep, row_block, p * (PANEL // BLOCK))
                part = jnp.dot(tile, right[at, :], preferred_element_type=jnp.float32)
                total[i, rows, :] = part if p == 0 else total[i, rows, :] + part
    for i, out in enumerate(outs):
        out[...] = total[i]


def sketch_parts(ks, place, keep_mask, weights, test_matrix):
    panels = WIDTH // PANEL
    scratch = [
        pltpu.SMEM((ROWS // BLOCK, WIDTH // BLOCK), jnp.int32),
        pltpu.VMEM((len(ks), QUARTER, WIDTH), jnp.bfloat16),
        pltpu.VMEM((len(ks), QUARTER, K), jnp.float32),
        pltpu.SemaphoreType.DMA,
        pltpu.SemaphoreType.DMA((panels, len(ks))),
    ]
    outs = [jax.ShapeDtypeStruct((QUARTER, K), jnp.float32)] * len(ks)
    return pl.pallas_call(
        lambda *refs: sketch_kernel(ks, *refs),
        in_specs=[SCALARS, FAR, FAR, WHOLE],
        out_specs=[WHOLE] * len(outs),
        scratch_shapes=scratch,
        out_shape=outs,
        compiler_params=pltpu.CompilerParams(vmem_limit_bytes=51 * MIB),
        cost_estimate=SMALL,
        name="sketch",
    )(place, keep_mask, weights, test_matrix)


def turn_kernel(rows, out):
    out[...] = rows[...].T


def turn(quarter):
    return pl.pallas_call(
        turn_kernel,
        in_specs=[WHOLE],
        out_specs=WHOLE,
        out_shape=jax.ShapeDtypeStruct((K, QUARTER), jnp.float32),
        compiler_params=pltpu.CompilerParams(vmem_limit_bytes=4 * MIB),
        cost_estimate=SMALL,
        name="turn",
    )(quarter)


def gram_pair(first, second):
    def square_of(piece):
        return lax.dot_general(
            piece[...], piece[...], (((1,), (1,)), ((), ())), precision=HIGHEST, preferred_element_type=jnp.float32
        )

    return square_of(first) + square_of(second)


def inverse_factor_kernel(mine, theirs, out, step=8):
    gram = mine[...] + theirs[...]
    lanes = lax.broadcasted_iota(jnp.int32, (K, K), 1)
    rows = lax.broadcasted_iota(jnp.int32, (K, K), 0)
    unit = jnp.where(lanes == rows, 1.0, 0.0).astype(jnp.float32)
    for top in range(0, K, step):
        left = K - top
        column = [jnp.broadcast_to(gram[:, top + i : top + i + 1], (left, K)) for i in range(step)]
        row = [gram[i : i + 1, :] for i in range(step)]
        side = [unit[i : i + 1, :] for i in range(step)]
        for i in range(step):
            pivot = column[i][i : i + 1, :]
            inverse = 1.0 / pivot
            for m in range(i + 1, step):
                factor = column[i][m : m + 1, :] * inverse
                column[m] = column[m] - column[i] * factor
                row[m] = row[m] - row[i] * factor
                side[m] = side[m] - side[i] * factor
            out[top + i : top + i + 1, :] = side[i] * lax.rsqrt(pivot)
            row[i] = row[i] * inverse
            side[i] = side[i] * inverse
        if left > step:
            gram, unit = gram[step:], unit[step:]
            for i in range(step):
                gram = gram - column[i][step:] * row[i]
                unit = unit - column[i][step:] * side[i]


def inverse_factor(mine, theirs):
    return pl.pallas_call(
        inverse_factor_kernel,
        in_specs=[WHOLE] * 2,
        out_specs=WHOLE,
        out_shape=jax.ShapeDtypeStruct((K, K), jnp.float32),
        compiler_params=pltpu.CompilerParams(vmem_limit_bytes=8 * MIB),
        cost_estimate=SMALL,
        name="inverse_factor",
    )(mine, theirs)


def quarter_column(place, near, own):
    chip = place[1] if near else 1 - place[1]
    core = place[2] if own else 1 - place[2]
    return (chip * 2 + core) * (WIDTH // 4 // BLOCK)


def quarter_copies(place, near, own, weights, tile, sems):
    copies = []
    for k in range(4):
        columns = pl.ds(pl.multiple_of(quarter_column(place, near, own) * BLOCK, BLOCK), WIDTH // 4)
        rows = pl.ds(pl.multiple_of((place[0] ^ ORDER[k]) * QUARTER, QUARTER), QUARTER)
        at = pl.ds(k * QUARTER, QUARTER)
        copies.append(pltpu.make_async_copy(weights.at[rows, columns], tile.at[at, :], sems.at[k]))
    return copies


def kept(place, near, own, k, tile, keep):
    rows = slice(k * QUARTER, (k + 1) * QUARTER)
    return masked(tile[rows, :], keep, (place[0] ^ ORDER[k]) * (QUARTER // BLOCK), quarter_column(place, near, own))


def stage_kernel(own, place, keep_mask, weights, ready, out, keep, keep_sem, sems):
    keep_copy = pltpu.make_async_copy(keep_mask, keep, keep_sem)
    keep_copy.start()
    copies = quarter_copies(place, False, own, weights, out, sems)
    for copy in copies:
        copy.start()
    keep_copy.wait()
    for k in range(4):
        copies[k].wait()
        out[k * QUARTER : (k + 1) * QUARTER, :] = kept(place, False, own, k, out, keep)


def stage(own, place, keep_mask, weights, ready):
    return pl.pallas_call(
        lambda *refs: stage_kernel(own, *refs),
        in_specs=[SCALARS, FAR, FAR, FAR],
        out_specs=WHOLE,
        out_shape=jax.ShapeDtypeStruct((ROWS, WIDTH // 4), jnp.bfloat16),
        scratch_shapes=[
            pltpu.SMEM((ROWS // BLOCK, WIDTH // BLOCK), jnp.int32),
            pltpu.SemaphoreType.DMA,
            pltpu.SemaphoreType.DMA((4,)),
        ],
        compiler_params=pltpu.CompilerParams(vmem_limit_bytes=46 * MIB),
        cost_estimate=SMALL,
        name="stage",
    )(place, keep_mask, weights, ready)


def two_terms(parts, sketch):
    for k, part in enumerate(parts):
        at = slice(k * QUARTER, (k + 1) * QUARTER)
        high = part[...].astype(jnp.bfloat16)
        sketch[0:K, at] = high
        sketch[K : 2 * K, at] = (part[...] - high.astype(jnp.float32)).astype(jnp.bfloat16)


def project(sketch, tile):
    both = jnp.dot(sketch[...], tile, preferred_element_type=jnp.float32)
    return both[:K] + both[K:]


def begin_kernel(mine, three, send_tile, stay_tile, gram, sketch, send, stay):
    two_terms((mine, three), sketch)
    gram[...] = gram_pair(mine, three)
    send[...] = project(sketch, send_tile[: 2 * QUARTER, :])
    stay[...] = project(sketch, stay_tile[: 2 * QUARTER, :])


def begin(mine, three, send_tile, stay_tile):
    return pl.pallas_call(
        begin_kernel,
        in_specs=[WHOLE] * 4,
        out_specs=[WHOLE] * 4,
        out_shape=[
            jax.ShapeDtypeStruct((K, K), jnp.float32),
            jax.ShapeDtypeStruct((2 * K, 2 * QUARTER), jnp.bfloat16),
            jax.ShapeDtypeStruct((K, WIDTH // 4), jnp.float32),
            jax.ShapeDtypeStruct((K, WIDTH // 4), jnp.float32),
        ],
        compiler_params=pltpu.CompilerParams(vmem_limit_bytes=16 * MIB),
        cost_estimate=SMALL,
        name="begin",
    )(mine, three, send_tile, stay_tile)


def first_kernel(one, two, gram, tile, before, out, sketch):
    two_terms((one, two), sketch)
    out[:, :CHUNK] = before[:, :CHUNK] + project(sketch, tile[2 * QUARTER :, :CHUNK])
    out[:, CHUNK:] = gram[...] + gram_pair(one, two)


def first_term(one, two, gram, tile, before):
    return pl.pallas_call(
        first_kernel,
        in_specs=[WHOLE] * 5,
        out_specs=[WHOLE] * 2,
        out_shape=[
            jax.ShapeDtypeStruct((K, CHUNK + K), jnp.float32),
            jax.ShapeDtypeStruct((2 * K, 2 * QUARTER), jnp.bfloat16),
        ],
        compiler_params=pltpu.CompilerParams(vmem_limit_bytes=16 * MIB),
        cost_estimate=SMALL,
        name="first",
    )(one, two, gram, tile, before)


def far_kernel(at, sketch, tile, before, out):
    out[...] = before[:, at] + project(sketch, tile[2 * QUARTER :, at])


def far_term(at, sketch, tile, before):
    return pl.pallas_call(
        lambda *refs: far_kernel(at, *refs),
        in_specs=[WHOLE] * 3,
        out_specs=WHOLE,
        out_shape=jax.ShapeDtypeStruct((K, at.stop - at.start), jnp.float32),
        compiler_params=pltpu.CompilerParams(vmem_limit_bytes=16 * MIB),
        cost_estimate=SMALL,
        name="far",
    )(sketch, tile, before)


def near_kernel(place, keep_mask, sketch_a, sketch_b, weights, *refs):
    outs, keep, tiles, keep_sem, sems = refs[:8], *refs[8:]
    keep_copy = pltpu.make_async_copy(keep_mask, keep, keep_sem)
    keep_copy.start()
    copies = [quarter_copies(place, True, i == 1, weights, tiles.at[i], sems.at[i]) for i in range(2)]
    for copy in copies[0] + copies[1]:
        copy.start()
    keep_copy.wait()
    for i in range(2):
        total = 0.0
        for k in range(4):
            copies[i][k].wait()
            sketch = (sketch_a, sketch_b)[k // 2].at[:, k % 2 * QUARTER : (k % 2 + 1) * QUARTER]
            total = total + project(sketch, kept(place, True, i == 1, k, tiles.at[i], keep))
        for t in range(4):
            outs[4 * i + t][...] = total[:, t * QUARTER : (t + 1) * QUARTER]


def near_terms(place, keep_mask, sketch_a, sketch_b, weights):
    return pl.pallas_call(
        near_kernel,
        in_specs=[SCALARS, FAR, WHOLE, WHOLE, FAR],
        out_specs=[WHOLE] * 8,
        scratch_shapes=[
            pltpu.SMEM((ROWS // BLOCK, WIDTH // BLOCK), jnp.int32),
            pltpu.VMEM((2, ROWS, WIDTH // 4), jnp.bfloat16),
            pltpu.SemaphoreType.DMA,
            pltpu.SemaphoreType.DMA((2, 4)),
        ],
        out_shape=[jax.ShapeDtypeStruct((K, QUARTER), jnp.float32)] * 8,
        compiler_params=pltpu.CompilerParams(vmem_limit_bytes=40 * MIB),
        cost_estimate=SMALL,
        name="near",
    )(place, keep_mask, sketch_a, sketch_b, weights)


def dot_split(left, right):
    def terms(x):
        high = x.astype(jnp.bfloat16)
        return high, (x - high.astype(jnp.float32)).astype(jnp.bfloat16)

    (a, b), (c, d) = terms(left), terms(right)
    return jnp.dot(
        jnp.concatenate([a, a, b], axis=1), jnp.concatenate([c, d, c], axis=0), preferred_element_type=jnp.float32
    )


def write_turned(inverse, columns, scale, out, held, sems):
    copies = []
    for t in range(4):
        value, place = columns(t)
        held[t] = (dot_split(inverse, value) * scale).T
        rows = pl.ds(pl.multiple_of(place * QUARTER, QUARTER), QUARTER)
        copies.append(pltpu.make_async_copy(held.at[t], out.at[rows, :], sems.at[t]))
        copies[-1].start()
    for copy in copies:
        copy.wait()


TURNED = dict(
    out_specs=FAR,
    out_shape=jax.ShapeDtypeStruct((ROWS, K), jnp.float32),
    scratch_shapes=[pltpu.VMEM((4, QUARTER, K), jnp.float32), pltpu.SemaphoreType.DMA((4,))],
    compiler_params=pltpu.CompilerParams(vmem_limit_bytes=16 * MIB),
    cost_estimate=SMALL,
)


def basis_kernel(place, inverse, *refs):
    parts, out, held, sems = refs[:4], *refs[4:]
    write_turned(inverse[...], lambda k: (parts[k][...], place[0] ^ k), math.sqrt(D), out, held, sems)


def range_basis_of(place, inverse, parts):
    return pl.pallas_call(basis_kernel, in_specs=[SCALARS] + [WHOLE] * 5, name="basis", **TURNED)(place, inverse, *parts)


def finish_kernel(inverse, far_a, far_b, *refs):
    terms, out, held, sems = refs[:8], *refs[8:]

    def columns(t):
        start, stop = t * QUARTER, (t + 1) * QUARTER
        far = [far_a[:, start : min(stop, CHUNK)]] if start < CHUNK else []
        far += [far_b[:, max(start, CHUNK) - CHUNK : stop - CHUNK]] if stop > CHUNK else []
        return terms[t][...] + terms[t + 4][...] + (far[0] if len(far) == 1 else jnp.concatenate(far, axis=1)), t

    write_turned(inverse[...], columns, 1.0, out, held, sems)


def finish(inverse, far, here, core):
    return pl.pallas_call(finish_kernel, in_specs=[WHOLE] * 11, name="finish", **TURNED)(inverse, *far, *here, *core)


def shards(weights, keep_mask, test_matrix):
    place = position()

    one, two, three = sketch_parts((1, 2, 3), place, keep_mask, weights, test_matrix)
    three, two, one = swap(three, square(True, 3)), swap(two, square(True, 2)), swap(one, square(True, 1))
    part = sketch_parts((0,), place, keep_mask, weights, test_matrix)[0] + three + two + one
    one, two, three = (swap(part, square(False, k)) for k in (1, 2, 3))
    send_tile = stage(False, place, keep_mask, weights, part)
    part, send_tile = lax.optimization_barrier(((part + two) + (one + three), send_tile))
    sent = swap(part, ACROSS)
    stay_tile = stage(True, place, keep_mask, weights, part)
    part, stay_tile = lax.optimization_barrier((part + sent, stay_tile))

    mine = turn(part)
    one, two, three = (swap(mine, square(True, k)) for k in (1, 2, 3))

    gram, sketch_a, send_a, stay_a = begin(mine, three, send_tile, stay_tile)
    send, sketch_b = first_term(one, two, gram, send_tile, send_a)
    early, late = slice(0, CHUNK), slice(CHUNK, WIDTH // 4)
    sent = swap(send, CORES)
    total = far_term(early, sketch_b, stay_tile, stay_a) + sent[:, :CHUNK]
    gram = send[:, CHUNK:] + sent[:, CHUNK:]
    far_a = swap(total, CHIPS)
    far_gram = swap(gram, OTHERS)
    rest = far_term(late, sketch_b, stay_tile, stay_a) + swap(far_term(late, sketch_b, send_tile, send_a), CORES)
    rest, gram, sketch_b = lax.optimization_barrier((rest, gram, sketch_b))
    far_b = swap(rest, CHIPS)
    terms = near_terms(place, keep_mask, sketch_a, sketch_b, weights)
    core = [swap(term, CORES) for term in terms[:4]]
    inverse = inverse_factor(gram, far_gram)
    basis = range_basis_of(place, inverse, (mine, one, two, three))
    return basis, finish(inverse, (far_a, far_b), terms[4:], core)


def solution(mesh):
    placed = (P("rep", "shard"), P("rep", "shard"), P("shard", None))
    return jax.shard_map(
        shards,
        mesh=mesh,
        in_specs=placed,
        out_specs=(P("rep", None), P(("shard", "rep"), None)),
        check_vma=False,
    )
```
